32 devices in a mesh: energy: 8 (over z, core), layer: 4 (over y, x).
Axes of the slice: x: 2, y: 2, z: 4, core: 2. Of those that a mesh axis runs over, the one named last changes fastest.
Arguments:
- green_local: bfloat16 [4, 16, 384, 2, 384], P('layer', 'energy'), may hold values from -6 to 6
- hopping: bfloat16 [4, 384, 2, 384], P('layer'), may hold values from -0.005859375 to 0.005859375
- coupling: bfloat16 [4, 384, 384], P('layer'), may hold values from -0.25 to 0.25
Outputs:
- green_full: bfloat16 [4, 16, 384, 2, 384], P('layer', 'energy')
The draws below stay inside these ranges and needn't reach their ends.
All inputs are finite; a program needn't handle non-finite values.
Results may differ from the reference program's by a relative error of at most 0.02.
Values may be sent and summed in bfloat16 or wider, within the bound.
A program may use at most 64 MiB of HBM per device.

```python
import jax
import jax.numpy as jnp
from jax import lax

ORB = 384
OFFSET = 2
ENERGIES = 16
LAYERS = 4


def block_scale(key, dims, shards, smallest, largest):
    def one(dim, shards_of):
        steps = jax.random.uniform(jax.random.fold_in(jax.random.fold_in(key, 6), dim), (shards_of,), jnp.float32, smallest / len(shards), largest / len(shards))
        return jnp.repeat(jnp.exp(steps), dims[dim] // shards_of).reshape((-1,) + (1,) * (len(dims) - dim - 1))

    factor_of = one(*shards[0])
    for cut in shards[1:]:
        factor_of = factor_of * one(*cut)
    return factor_of


def centred(own_key, extent, spread, most, cuts=(), dtype=jnp.bfloat16):
    factor_of = block_scale(own_key, extent, cuts, -0.22, 0.18) if cuts else 1.0
    entries = jax.random.normal(own_key, extent, jnp.float32) * spread * factor_of
    return jnp.minimum(jnp.maximum(entries, -most), most).astype(dtype)


def setup_inputs(seed: int = 0) -> dict:
    streams_of = jax.random.split(jax.random.key(seed), 4)
    return {
        "green_local": centred(streams_of[0], (LAYERS, ENERGIES, ORB, 2, ORB), 1.0, 6.0, ((0, 4), (1, 8))),
        "hopping": centred(streams_of[1], (LAYERS, ORB, 2, ORB), (ORB * ORB * 19 // 3) ** -0.5, 0.005859375, ((0, 4),)),
        "coupling": centred(streams_of[2], (LAYERS, ORB, ORB), (ORB * 7 // 5) ** -0.5, 0.25, ((0, 4),)),
    }


def expand(blocks):
    real_part = blocks[..., :, 0, :]
    imag_part = blocks[..., :, 1, :]
    upper_half = jnp.concatenate([real_part, imag_part], axis=-1)
    lower_half = jnp.concatenate([-imag_part, real_part], axis=-1)
    return jnp.concatenate([upper_half, lower_half], axis=-2)


def complex_product(left_block, right_block):
    row_blocks = left_block.astype(jnp.float32).reshape(left_block.shape[:-2] + (2 * left_block.shape[-1],))
    product_rows = jnp.matmul(row_blocks, expand(right_block.astype(jnp.float32)), precision=lax.Precision.HIGHEST)
    return product_rows.reshape(left_block.shape)


def partner_sum(following):
    padded = jnp.pad(following.astype(jnp.float32), ((OFFSET, OFFSET), (0, 0), (0, 0), (0, 0)))
    count = following.shape[0]
    return (padded[2 * OFFSET:] + padded[:count]).astype(jnp.bfloat16)


def reference(green_local, hopping, coupling):
    layer_count = green_local.shape[0]
    following = green_local[layer_count - 1]
    results = [None] * layer_count
    for layer_index in range(layer_count - 1, -1, -1):
        isolated = green_local[layer_index]
        phonon = coupling[layer_index].astype(jnp.float32)
        coupled = complex_product(isolated, hopping[layer_index]).astype(jnp.bfloat16)
        partner = partner_sum(following)
        scatter_left = jnp.einsum("ij,ejcl->eicl", phonon, partner.astype(jnp.float32), precision=lax.Precision.HIGHEST).astype(jnp.bfloat16)
        combined = (following.astype(jnp.float32) + jnp.matmul(scatter_left.astype(jnp.float32), phonon.T, precision=lax.Precision.HIGHEST)).astype(jnp.bfloat16)
        product = complex_product(coupled, combined).astype(jnp.bfloat16)
        flipped = jnp.transpose(coupled, (0, 3, 2, 1))
        following = (isolated.astype(jnp.float32) + complex_product(product, flipped)).astype(jnp.bfloat16)
        results[layer_index] = following
    return jnp.stack(results)
```

```python
import functools

import jax
import jax.numpy as jnp
from jax import lax
from jax.experimental import pallas as pl
from jax.experimental.pallas import tpu as pltpu
from jax.sharding import PartitionSpec as P

MESH = pl.DeviceIdType.MESH
F32 = jnp.float32
BF16 = jnp.bfloat16


def routes(layers, energies):
    if layers == 4 and energies == 2:
        return [
            (0, (3, 2)),
            (1, (3, 1, 0, 2)),
            (0, (2, 3, 1)),
            (1, (2, 0, 1)),
            (0, (1, 0)),
            (1, (1, 3, 2, 0)),
        ]
    return [(i, (l, l - 1)) for l in range(layers - 1, 0, -1) for i in range(energies)]


def kernel(
    dims, streams, slots,
    g_ref, h_ref, c_ref, out_ref,
    fin, halo, relay, right, left, mid,
    fin_sem, halo_sem, relay_sem, out_send, halo_send, relay_send,
):
    layers, rows_of, energies, chunks, rows, size, group = dims
    me = lax.axis_index("layer")
    d = lax.axis_index("energy")
    has_low, has_high = d > 0, d < rows_of - 1
    top = me == layers - 1

    pairs = sorted({tuple(sorted(p)) for _, path in streams for p in zip(path, path[1:])})
    barrier = pltpu.get_barrier_semaphore()
    count = has_low.astype(jnp.int32) + has_high.astype(jnp.int32)
    for l in range(layers):
        partners = [b if a == l else a for a, b in pairs if l in (a, b)]

        @pl.when(me == l)
        def _(partners=partners):
            for other in partners:
                pl.semaphore_signal(barrier, inc=1, device_id={"layer": other}, device_id_type=MESH)

        count = count + jnp.where(me == l, len(partners), 0)

    @pl.when(has_low)
    def _():
        pl.semaphore_signal(barrier, inc=1, device_id={"energy": d - 1}, device_id_type=MESH)

    @pl.when(has_high)
    def _():
        pl.semaphore_signal(barrier, inc=1, device_id={"energy": d + 1}, device_id_type=MESH)

    pl.semaphore_wait(barrier, count)

    def halo_copy(src, side, i, c):
        return pltpu.make_async_remote_copy(
            src_ref=src.at[i, c], dst_ref=halo.at[side, i, c],
            send_sem=halo_send.at[side, i, c], recv_sem=halo_sem.at[side, i, c],
            device_id={"energy": d + 1 if side == 0 else d - 1}, device_id_type=MESH,
        )

    def forward(src, i, c):
        @pl.when(has_high)
        def _():
            halo_copy(src, 0, i, c).start()

        @pl.when(has_low)
        def _():
            halo_copy(src, 1, i, c).start()

    def stream_copy(s, hop, c):
        i, path = streams[s]
        target = path[hop + 1]
        if hop == 0:
            src, send = out_ref.at[i, c], out_send.at[i, c]
        else:
            src, send = relay.at[slots[s], c], relay_send.at[slots[s], c]
        if hop == len(path) - 2:
            dst, recv = fin.at[i, c], fin_sem.at[i, c]
        else:
            dst, recv = relay.at[slots[s], c], relay_sem.at[slots[s], c]
        return pltpu.make_async_remote_copy(
            src_ref=src, dst_ref=dst, send_sem=send, recv_sem=recv,
            device_id={"layer": target}, device_id_type=MESH,
        )

    def pass_on(s, hop):
        def body(c, carry):
            stream_copy(s, hop - 1, c).wait_recv()
            stream_copy(s, hop, c).start()
            return carry

        lax.fori_loop(0, chunks, body, 0)

    @pl.when(top)
    def _():
        def body(c, carry):
            for i in range(energies):
                forward(g_ref, i, c)
            return carry

        lax.fori_loop(0, chunks, body, 0)
        fin[...] = g_ref[...]

    @pl.when(d == 0)
    def _():
        halo[0] = jnp.zeros_like(halo[0])

    @pl.when(d == rows_of - 1)
    def _():
        halo[1] = jnp.zeros_like(halo[1])

    hop_r, hop_i = h_ref[:, :size], h_ref[:, size:]
    mid[0, :size, :] = h_ref[...]
    mid[0, size : 2 * size, :size] = -hop_i
    mid[0, size : 2 * size, size:] = hop_r
    for i in range(energies):
        blocks = g_ref[i].reshape(size, 2 * size)
        left[i, :, : 2 * size] = jnp.dot(
            blocks, mid[0, : 2 * size, :], preferred_element_type=F32
        ).astype(BF16)
    for i in range(energies):
        for part in range(2):
            factor = left[i, :, part * size : (part + 1) * size]
            left[i, :, (2 + part) * size : (3 + part) * size] = jnp.dot(
                factor, c_ref[...], preferred_element_type=F32
            ).astype(BF16)
        for which in range(2):
            start = 2 * which * size
            flip_r = left[i, :, start : start + size].T
            flip_i = left[i, :, start + size : start + 2 * size].T
            right[i, which, :size, :size] = flip_r
            right[i, which, :size, size:] = flip_i
            right[i, which, size:, :size] = -flip_i
            right[i, which, size:, size:] = flip_r

    def relays(when):
        for l in range(layers):
            jobs = [
                (s, hop)
                for s, (_, path) in enumerate(streams)
                for hop, node in enumerate(path[1:-1], 1)
                if node == l and (path[0] > l + 1 if when == "before" else path[0] <= l)
            ]
            if jobs:
                @pl.when(me == l)
                def _(jobs=jobs):
                    for s, hop in jobs:
                        pass_on(s, hop)

    relays("before")

    def expand_into(i, which, c, value):
        value = value.astype(BF16)
        base = which * 2 * size + c * rows
        mid[i, pl.ds(pl.multiple_of(base, 16), rows), :] = value
        low = pl.ds(pl.multiple_of(base + size, 16), rows)
        mid[i, low, :size] = -value[:, size:]
        mid[i, low, size:] = value[:, :size]

    lags = []
    for i in range(energies):
        lag = jnp.int32(0)
        for l in range(layers - 1):
            hops = {e: len(path) for e, path in streams if path[-1] == l}
            lag = lag + jnp.where(me == l, hops[i] - min(hops.values()), 0)
        lags.append(lag)
    worst = max(len(path) for _, path in streams) - 2

    def step(t, carry):
        for i in range(energies):
            c = t - lags[i]

            @pl.when((c >= 0) & (c < chunks) & jnp.logical_not(top))
            def _(i=i, c=c):
                pltpu.make_async_remote_copy(
                    src_ref=fin.at[i, c], dst_ref=fin.at[i, c],
                    send_sem=out_send.at[i, c], recv_sem=fin_sem.at[i, c],
                    device_id={"layer": me + 1}, device_id_type=MESH,
                ).wait_recv()
                forward(fin, i, c)

        for i in range(energies):
            c = t - lags[i]

            @pl.when((c >= 0) & (c < chunks))
            def _(i=i, c=c):
                expand_into(i, 0, c, jnp.dot(fin[i, c], right[i, 0], preferred_element_type=F32))

        for i in range(energies):
            c = t - lags[i] - 1

            @pl.when((c >= 0) & (c < chunks))
            def _(i=i, c=c):
                @pl.when(has_low)
                def _():
                    halo_copy(fin, 0, i, c).wait_recv()

                @pl.when(has_high)
                def _():
                    halo_copy(fin, 1, i, c).wait_recv()

                partner = (halo[0, i, c].astype(F32) + halo[1, i, c].astype(F32)).astype(BF16)
                expand_into(i, 1, c, jnp.dot(partner, right[i, 1], preferred_element_type=F32))

        return carry

    lax.fori_loop(0, chunks + 1 + worst, step, 0)

    def finish(k, carry):
        for i in range(energies):
            base = pl.multiple_of(k * (group * rows), 16)
            total = jnp.dot(
                left[i, pl.ds(base, group * rows), :], mid[i], preferred_element_type=F32
            )
            for j in range(group):
                c = k * group + j
                out_ref[i, c] = (
                    g_ref[i, c].astype(F32) + total[j * rows : (j + 1) * rows]
                ).astype(BF16)
            for s, (e, path) in enumerate(streams):
                if e == i:
                    @pl.when(me == path[0])
                    def _(s=s):
                        for j in range(group):
                            stream_copy(s, 0, k * group + j).start()
        return carry

    lax.fori_loop(0, chunks // group, finish, 0)
    relays("after")

    def drain(c, carry):
        for s, (_, path) in enumerate(streams):
            for hop, node in enumerate(path[:-1]):
                @pl.when(me == node)
                def _(s=s, hop=hop):
                    stream_copy(s, hop, c).wait_send()
        for i in range(energies):
            @pl.when(has_high)
            def _(i=i):
                halo_copy(fin, 0, i, c).wait_send()

            @pl.when(has_low)
            def _(i=i):
                halo_copy(fin, 1, i, c).wait_send()
        return carry

    lax.fori_loop(0, chunks, drain, 0)


def per_device(green_local, hopping, coupling):
    _, energies, size, _, _ = green_local.shape
    layers, rows_of = lax.axis_size("layer"), lax.axis_size("energy")
    rows = 64 if size % 64 == 0 else 16
    chunks = size // rows
    group = 2 if chunks % 2 == 0 else 1
    streams = routes(layers, energies)
    slots, relayed = {}, 0
    for s, (_, path) in enumerate(streams):
        if len(path) > 2:
            slots[s] = relayed
            relayed += 1
    relayed = max(relayed, 1)
    block = (energies, chunks, rows, 2 * size)
    sem = pltpu.SemaphoreType.DMA
    vmem = pl.BlockSpec(memory_space=pltpu.VMEM)
    result = pl.pallas_call(
        functools.partial(
            kernel, (layers, rows_of, energies, chunks, rows, size, group), streams, slots
        ),
        out_shape=jax.ShapeDtypeStruct(block, BF16),
        in_specs=[vmem] * 3,
        out_specs=vmem,
        scratch_shapes=[
            pltpu.VMEM(block, BF16),
            pltpu.VMEM((2,) + block, BF16),
            pltpu.VMEM((relayed,) + block[1:], BF16),
            pltpu.VMEM((energies, 2, 2 * size, 2 * size), BF16),
            pltpu.VMEM((energies, size, 4 * size), BF16),
            pltpu.VMEM((energies, 4 * size, 2 * size), BF16),
            sem((energies, chunks)),
            sem((2, energies, chunks)),
            sem((relayed, chunks)),
            sem((energies, chunks)),
            sem((2, energies, chunks)),
            sem((relayed, chunks)),
        ],
        compiler_params=pltpu.CompilerParams(
            collective_id=0, has_side_effects=True, vmem_limit_bytes=48 * 2**20
        ),
        name="sweep",
    )(
        green_local.reshape(block),
        hopping.reshape(size, 2 * size),
        coupling.reshape(size, size),
    )
    return result.reshape(green_local.shape)


def solution(mesh):
    placed = (
        P("layer", "energy", None, None, None),
        P("layer", None, None, None),
        P("layer", None, None),
    )
    return jax.shard_map(
        per_device,
        mesh=mesh,
        in_specs=placed,
        out_specs=P("layer", "energy", None, None, None),
        check_vma=False,
    )
```

```python
import functools

import jax
import jax.numpy as jnp
from jax import lax
from jax.experimental import pallas as pl
from jax.experimental.pallas import tpu as pltpu
from jax.sharding import PartitionSpec as P

MESH = pl.DeviceIdType.MESH
F32 = jnp.float32
BF16 = jnp.bfloat16


def routes(layers, energies, chunks):
    if layers == 4 and energies == 2:
        cut = chunks - chunks // 6
        return [
            (0, 0, chunks, (3, 2)),
            (1, 0, cut, (3, 1, 0, 2)),
            (1, cut, chunks, (3, 2)),
            (0, 0, chunks, (2, 3, 1)),
            (1, 0, chunks, (2, 0, 1)),
            (0, 0, chunks, (1, 0)),
            (1, 0, cut, (1, 3, 2, 0)),
            (1, cut, chunks, (1, 0)),
        ]
    return [(i, 0, chunks, (l, l - 1)) for l in range(layers - 1, 0, -1) for i in range(energies)]


def kernel(
    dims, streams, slots,
    g_ref, h_ref, c_ref, out_ref,
    fin, halo, relay, right, left, hops, total,
    fin_sem, halo_sem, relay_sem, out_send, halo_send, relay_send,
):
    layers, rows_of, energies, chunks, rows, size, group = dims
    blocks, deep = chunks // group, group * rows
    me = lax.axis_index("layer")
    d = lax.axis_index("energy")
    has_low, has_high = d > 0, d < rows_of - 1
    top = me == layers - 1

    pairs = sorted({tuple(sorted(p)) for _, _, _, path in streams for p in zip(path, path[1:])})
    barrier = pltpu.get_barrier_semaphore()
    count = has_low.astype(jnp.int32) + has_high.astype(jnp.int32)
    for l in range(layers):
        partners = [b if a == l else a for a, b in pairs if l in (a, b)]

        @pl.when(me == l)
        def _(partners=partners):
            for other in partners:
                pl.semaphore_signal(barrier, inc=1, device_id={"layer": other}, device_id_type=MESH)

        count = count + jnp.where(me == l, len(partners), 0)

    @pl.when(has_low)
    def _():
        pl.semaphore_signal(barrier, inc=1, device_id={"energy": d - 1}, device_id_type=MESH)

    @pl.when(has_high)
    def _():
        pl.semaphore_signal(barrier, inc=1, device_id={"energy": d + 1}, device_id_type=MESH)

    pl.semaphore_wait(barrier, count)

    def halo_copy(src, side, i, c):
        return pltpu.make_async_remote_copy(
            src_ref=src.at[i, c], dst_ref=halo.at[side, i, c],
            send_sem=halo_send.at[side, i, c], recv_sem=halo_sem.at[side, i, c],
            device_id={"energy": d + 1 if side == 0 else d - 1}, device_id_type=MESH,
        )

    def forward(src, i, c):
        @pl.when(has_high)
        def _():
            halo_copy(src, 0, i, c).start()

        @pl.when(has_low)
        def _():
            halo_copy(src, 1, i, c).start()

    def stream_copy(s, hop, c):
        i, _, _, path = streams[s]
        target = path[hop + 1]
        if hop == 0:
            src, send = out_ref.at[i, c], out_send.at[i, c]
        else:
            src, send = relay.at[slots[s], c], relay_send.at[slots[s], c]
        if hop == len(path) - 2:
            dst, recv = fin.at[i, c], fin_sem.at[i, c]
        else:
            dst, recv = relay.at[slots[s], c], relay_sem.at[slots[s], c]
        return pltpu.make_async_remote_copy(
            src_ref=src, dst_ref=dst, send_sem=send, recv_sem=recv,
            device_id={"layer": target}, device_id_type=MESH,
        )

    def pass_on(s, hop):
        def body(c, carry):
            stream_copy(s, hop - 1, c).wait_recv()
            stream_copy(s, hop, c).start()
            return carry

        lax.fori_loop(streams[s][1], streams[s][2], body, 0)

    @pl.when(top)
    def _():
        def body(c, carry):
            for i in range(energies):
                forward(g_ref, i, c)
            return carry

        lax.fori_loop(0, chunks, body, 0)
        fin[...] = g_ref[...]

    @pl.when(d == 0)
    def _():
        halo[0] = jnp.zeros_like(halo[0])

    @pl.when(d == rows_of - 1)
    def _():
        halo[1] = jnp.zeros_like(halo[1])

    hop_r, hop_i = h_ref[:, :size], h_ref[:, size:]
    hops[:size, :] = h_ref[...]
    hops[size:, :size] = -hop_i
    hops[size:, size:] = hop_r
    for i in range(energies):
        full = g_ref[i].reshape(size, 2 * size)
        total[i] = full.astype(F32)
        coupled = jnp.dot(full, hops[...], preferred_element_type=F32).astype(BF16)
        parts = [coupled[:, :size], coupled[:, size:]]
        for which in range(2):
            if which == 1:
                parts = [
                    jnp.dot(part, c_ref[...], preferred_element_type=F32).astype(BF16)
                    for part in parts
                ]
            for j in range(blocks):
                for part in range(2):
                    left[i, which, j, :, part * deep : (part + 1) * deep] = parts[part][
                        :, j * deep : (j + 1) * deep
                    ]
            flip_r, flip_i = parts[0].T, parts[1].T
            right[i, which, :size, :size] = flip_r
            right[i, which, :size, size:] = flip_i
            right[i, which, size:, :size] = -flip_i
            right[i, which, size:, size:] = flip_r

    def relays(when):
        for l in range(layers):
            jobs = [
                (s, hop)
                for s, (_, _, _, path) in enumerate(streams)
                for hop, node in enumerate(path[1:-1], 1)
                if node == l and (path[0] > l + 1 if when == "before" else path[0] <= l)
            ]
            if jobs:
                @pl.when(me == l)
                def _(jobs=jobs):
                    for s, hop in jobs:
                        pass_on(s, hop)

    relays("before")

    def add_block(i, which, j, value):
        mid = jnp.dot(value, right[i, which], preferred_element_type=F32).astype(BF16)
        swapped = jnp.concatenate([-mid[:, size:], mid[:, :size]], axis=1)
        both = jnp.concatenate([mid, swapped], axis=0)
        total[i] += jnp.dot(left[i, which, j], both, preferred_element_type=F32)

    def block_of(ref, j):
        return ref[pl.ds(j * group, group)].reshape(deep, 2 * size)

    lags = []
    for i in range(energies):
        lag = jnp.int32(0)
        for l in range(layers - 1):
            hops_of = {e: len(path) for e, lo, _, path in streams if path[-1] == l and lo == 0}
            late = 1 if hops_of[i] > min(hops_of.values()) else 0
            lag = lag + jnp.where(me == l, late, 0)
        lags.append(lag)
    worst = 1 if any(len(path) > 2 for _, _, _, path in streams) else 0

    def step(t, carry):
        for sub in range(group):
            for i in range(energies):
                j = t - lags[i]

                @pl.when((j >= 0) & (j < blocks) & jnp.logical_not(top))
                def _(i=i, j=j, sub=sub):
                    c = j * group + sub
                    pltpu.make_async_remote_copy(
                        src_ref=fin.at[i, c], dst_ref=fin.at[i, c],
                        send_sem=out_send.at[i, c], recv_sem=fin_sem.at[i, c],
                        device_id={"layer": me + 1}, device_id_type=MESH,
                    ).wait_recv()
                    forward(fin, i, c)

        for i in range(energies):
            j = t - lags[i]

            @pl.when((j >= 0) & (j < blocks))
            def _(i=i, j=j):
                add_block(i, 0, j, block_of(fin.at[i], j))

        for i in range(energies):
            j = t - lags[i] - 1

            @pl.when((j >= 0) & (j < blocks))
            def _(i=i, j=j):
                for sub in range(group):
                    @pl.when(has_low)
                    def _(sub=sub):
                        halo_copy(fin, 0, i, j * group + sub).wait_recv()

                    @pl.when(has_high)
                    def _(sub=sub):
                        halo_copy(fin, 1, i, j * group + sub).wait_recv()

                partner = block_of(halo.at[0, i], j).astype(F32) + block_of(
                    halo.at[1, i], j
                ).astype(F32)
                add_block(i, 1, j, partner.astype(BF16))

        return carry

    lax.fori_loop(0, blocks + 1 + worst, step, 0)

    def finish(c, carry):
        for i in reversed(range(energies)):
            out_ref[i, c] = total[i, pl.ds(pl.multiple_of(c * rows, 16), rows), :].astype(BF16)
            for s, (e, first, end, path) in enumerate(streams):
                if e == i:
                    @pl.when((me == path[0]) & (c >= first) & (c < end))
                    def _(s=s):
                        stream_copy(s, 0, c).start()
        return carry

    lax.fori_loop(0, chunks, finish, 0)
    relays("after")

    def drain(c, carry):
        for s, (_, first, end, path) in enumerate(streams):
            for hop, node in enumerate(path[:-1]):
                @pl.when((me == node) & (c >= first) & (c < end))
                def _(s=s, hop=hop):
                    stream_copy(s, hop, c).wait_send()
        for i in range(energies):
            @pl.when(has_high)
            def _(i=i):
                halo_copy(fin, 0, i, c).wait_send()

            @pl.when(has_low)
            def _(i=i):
                halo_copy(fin, 1, i, c).wait_send()
        return carry

    lax.fori_loop(0, chunks, drain, 0)


def per_device(green_local, hopping, coupling):
    _, energies, size, _, _ = green_local.shape
    layers, rows_of = lax.axis_size("layer"), lax.axis_size("energy")
    rows = 32 if size % 32 == 0 else 16
    chunks = size // rows
    group = 128 // rows if size % 128 == 0 else 1
    streams = routes(layers, energies, chunks)
    slots, relayed = {}, 0
    for s, (_, _, _, path) in enumerate(streams):
        if len(path) > 2:
            slots[s] = relayed
            relayed += 1
    relayed = max(relayed, 1)
    block = (energies, chunks, rows, 2 * size)
    sem = pltpu.SemaphoreType.DMA
    vmem = pl.BlockSpec(memory_space=pltpu.VMEM)
    result = pl.pallas_call(
        functools.partial(
            kernel, (layers, rows_of, energies, chunks, rows, size, group), streams, slots
        ),
        out_shape=jax.ShapeDtypeStruct(block, BF16),
        in_specs=[vmem] * 3,
        out_specs=vmem,
        scratch_shapes=[
            pltpu.VMEM(block, BF16),
            pltpu.VMEM((2,) + block, BF16),
            pltpu.VMEM((relayed,) + block[1:], BF16),
            pltpu.VMEM((energies, 2, 2 * size, 2 * size), BF16),
            pltpu.VMEM((energies, 2, chunks // group, size, 2 * group * rows), BF16),
            pltpu.VMEM((2 * size, 2 * size), BF16),
            pltpu.VMEM((energies, size, 2 * size), F32),
            sem((energies, chunks)),
            sem((2, energies, chunks)),
            sem((relayed, chunks)),
            sem((energies, chunks)),
            sem((2, energies, chunks)),
            sem((relayed, chunks)),
        ],
        compiler_params=pltpu.CompilerParams(
            collective_id=0, has_side_effects=True, vmem_limit_bytes=48 * 2**20
        ),
        name="sweep",
    )(
        green_local.reshape(block),
        hopping.reshape(size, 2 * size),
        coupling.reshape(size, size),
    )
    return result.reshape(green_local.shape)


def solution(mesh):
    placed = (
        P("layer", "energy", None, None, None),
        P("layer", None, None, None),
        P("layer", None, None),
    )
    return jax.shard_map(
        per_device,
        mesh=mesh,
        in_specs=placed,
        out_specs=P("layer", "energy", None, None, None),
        check_vma=False,
    )
```

```python
import functools

import jax
import jax.numpy as jnp
from jax import lax
from jax.experimental import pallas as pl
from jax.experimental.pallas import tpu as pltpu
from jax.sharding import PartitionSpec as P

MESH = pl.DeviceIdType.MESH
F32 = jnp.float32
BF16 = jnp.bfloat16


def routes(layers, energies, chunks):
    return [(i, 0, chunks, (l, l - 1)) for l in range(layers - 1, 0, -1) for i in range(energies)]


def kernel(
    dims, streams, slots,
    g_ref, h_ref, c_ref, out_ref,
    fin, halo, relay, right, left, hops, total,
    fin_sem, halo_sem, relay_sem, out_send, halo_send, relay_send,
):
    layers, rows_of, energies, chunks, rows, size, group = dims
    blocks, deep = chunks // group, group * rows
    me = lax.axis_index("layer")
    d = lax.axis_index("energy")
    has_low, has_high = d > 0, d < rows_of - 1
    top = me == layers - 1

    pairs = sorted({tuple(sorted(p)) for _, _, _, path in streams for p in zip(path, path[1:])})
    barrier = pltpu.get_barrier_semaphore()
    count = has_low.astype(jnp.int32) + has_high.astype(jnp.int32)
    for l in range(layers):
        partners = [b if a == l else a for a, b in pairs if l in (a, b)]

        @pl.when(me == l)
        def _(partners=partners):
            for other in partners:
                pl.semaphore_signal(barrier, inc=1, device_id={"layer": other}, device_id_type=MESH)

        count = count + jnp.where(me == l, len(partners), 0)

    @pl.when(has_low)
    def _():
        pl.semaphore_signal(barrier, inc=1, device_id={"energy": d - 1}, device_id_type=MESH)

    @pl.when(has_high)
    def _():
        pl.semaphore_signal(barrier, inc=1, device_id={"energy": d + 1}, device_id_type=MESH)

    pl.semaphore_wait(barrier, count)

    def halo_copy(src, side, i, c):
        return pltpu.make_async_remote_copy(
            src_ref=src.at[i, c], dst_ref=halo.at[side, i, c],
            send_sem=halo_send.at[side, i, c], recv_sem=halo_sem.at[side, i, c],
            device_id={"energy": d + 1 if side == 0 else d - 1}, device_id_type=MESH,
        )

    def forward(src, i, c):
        @pl.when(has_high)
        def _():
            halo_copy(src, 0, i, c).start()

        @pl.when(has_low)
        def _():
            halo_copy(src, 1, i, c).start()

    def stream_copy(s, hop, c):
        i, _, _, path = streams[s]
        target = path[hop + 1]
        if hop == 0:
            src, send = out_ref.at[i, c], out_send.at[i, c]
        else:
            src, send = relay.at[slots[s], c], relay_send.at[slots[s], c]
        if hop == len(path) - 2:
            dst, recv = fin.at[i, c], fin_sem.at[i, c]
        else:
            dst, recv = relay.at[slots[s], c], relay_sem.at[slots[s], c]
        return pltpu.make_async_remote_copy(
            src_ref=src, dst_ref=dst, send_sem=send, recv_sem=recv,
            device_id={"layer": target}, device_id_type=MESH,
        )

    def pass_on(s, hop):
        def body(c, carry):
            stream_copy(s, hop - 1, c).wait_recv()
            stream_copy(s, hop, c).start()
            return carry

        lax.fori_loop(streams[s][1], streams[s][2], body, 0)

    @pl.when(top)
    def _():
        def body(c, carry):
            for i in range(energies):
                forward(g_ref, i, c)
            return carry

        lax.fori_loop(0, chunks, body, 0)
        fin[...] = g_ref[...]

    @pl.when(d == 0)
    def _():
        halo[0] = jnp.zeros_like(halo[0])

    @pl.when(d == rows_of - 1)
    def _():
        halo[1] = jnp.zeros_like(halo[1])

    hop_r, hop_i = h_ref[:, :size], h_ref[:, size:]
    hops[:size, :] = h_ref[...]
    hops[size:, :size] = -hop_i
    hops[size:, size:] = hop_r
    for i in range(energies):
        full = g_ref[i].reshape(size, 2 * size)
        total[i] = full.astype(F32)
        coupled = jnp.dot(full, hops[...], preferred_element_type=F32).astype(BF16)
        parts = [coupled[:, :size], coupled[:, size:]]
        for which in range(2):
            if which == 1:
                parts = [
                    jnp.dot(part, c_ref[...], preferred_element_type=F32).astype(BF16)
                    for part in parts
                ]
            for j in range(blocks):
                for part in range(2):
                    left[i, which, j, :, part * deep : (part + 1) * deep] = parts[part][
                        :, j * deep : (j + 1) * deep
                    ]
            flip_r, flip_i = parts[0].T, parts[1].T
            right[i, which, :size, :size] = flip_r
            right[i, which, :size, size:] = flip_i
            right[i, which, size:, :size] = -flip_i
            right[i, which, size:, size:] = flip_r

    def relays(when):
        for l in range(layers):
            jobs = [
                (s, hop)
                for s, (_, _, _, path) in enumerate(streams)
                for hop, node in enumerate(path[1:-1], 1)
                if node == l and (path[0] > l + 1 if when == "before" else path[0] <= l)
            ]
            if jobs:
                @pl.when(me == l)
                def _(jobs=jobs):
                    for s, hop in jobs:
                        pass_on(s, hop)

    relays("before")

    def add_block(i, which, j, value):
        mid = jnp.dot(value, right[i, which], preferred_element_type=F32).astype(BF16)
        swapped = jnp.concatenate([-mid[:, size:], mid[:, :size]], axis=1)
        both = jnp.concatenate([mid, swapped], axis=0)
        total[i] += jnp.dot(left[i, which, j], both, preferred_element_type=F32)

    def block_of(ref, j):
        return ref[pl.ds(j * group, group)].reshape(deep, 2 * size)

    lags = []
    for i in range(energies):
        lag = jnp.int32(0)
        for l in range(layers - 1):
            hops_of = {e: len(path) for e, lo, _, path in streams if path[-1] == l and lo == 0}
            late = 1 if hops_of[i] > min(hops_of.values()) else 0
            lag = lag + jnp.where(me == l, late, 0)
        lags.append(lag)
    worst = 1 if any(len(path) > 2 for _, _, _, path in streams) else 0

    def step(t, carry):
        for sub in range(group):
            for i in range(energies):
                j = t - lags[i]

                @pl.when((j >= 0) & (j < blocks) & jnp.logical_not(top))
                def _(i=i, j=j, sub=sub):
                    c = j * group + sub
                    pltpu.make_async_remote_copy(
                        src_ref=fin.at[i, c], dst_ref=fin.at[i, c],
                        send_sem=out_send.at[i, c], recv_sem=fin_sem.at[i, c],
                        device_id={"layer": me + 1}, device_id_type=MESH,
                    ).wait_recv()
                    forward(fin, i, c)

        for i in range(energies):
            j = t - lags[i]

            @pl.when((j >= 0) & (j < blocks))
            def _(i=i, j=j):
                add_block(i, 0, j, block_of(fin.at[i], j))

        for i in range(energies):
            j = t - lags[i] - 1

            @pl.when((j >= 0) & (j < blocks))
            def _(i=i, j=j):
                for sub in range(group):
                    @pl.when(has_low)
                    def _(sub=sub):
                        halo_copy(fin, 0, i, j * group + sub).wait_recv()

                    @pl.when(has_high)
                    def _(sub=sub):
                        halo_copy(fin, 1, i, j * group + sub).wait_recv()

                partner = block_of(halo.at[0, i], j).astype(F32) + block_of(
                    halo.at[1, i], j
                ).astype(F32)
                add_block(i, 1, j, partner.astype(BF16))

        return carry

    lax.fori_loop(0, blocks + 1 + worst, step, 0)

    def finish(c, carry):
        for i in reversed(range(energies)):
            out_ref[i, c] = total[i, pl.ds(pl.multiple_of(c * rows, 16), rows), :].astype(BF16)
            for s, (e, first, end, path) in enumerate(streams):
                if e == i:
                    @pl.when((me == path[0]) & (c >= first) & (c < end))
                    def _(s=s):
                        stream_copy(s, 0, c).start()
        return carry

    lax.fori_loop(0, chunks, finish, 0)
    relays("after")

    def drain(c, carry):
        for s, (_, first, end, path) in enumerate(streams):
            for hop, node in enumerate(path[:-1]):
                @pl.when((me == node) & (c >= first) & (c < end))
                def _(s=s, hop=hop):
                    stream_copy(s, hop, c).wait_send()
        for i in range(energies):
            @pl.when(has_high)
            def _(i=i):
                halo_copy(fin, 0, i, c).wait_send()

            @pl.when(has_low)
            def _(i=i):
                halo_copy(fin, 1, i, c).wait_send()
        return carry

    lax.fori_loop(0, chunks, drain, 0)


def per_device(green_local, hopping, coupling):
    _, energies, size, _, _ = green_local.shape
    layers, rows_of = lax.axis_size("layer"), lax.axis_size("energy")
    rows = 32 if size % 32 == 0 else 16
    chunks = size // rows
    group = 128 // rows if size % 128 == 0 else 1
    streams = routes(layers, energies, chunks)
    slots, relayed = {}, 0
    for s, (_, _, _, path) in enumerate(streams):
        if len(path) > 2:
            slots[s] = relayed
            relayed += 1
    relayed = max(relayed, 1)
    block = (energies, chunks, rows, 2 * size)
    sem = pltpu.SemaphoreType.DMA
    vmem = pl.BlockSpec(memory_space=pltpu.VMEM)
    result = pl.pallas_call(
        functools.partial(
            kernel, (layers, rows_of, energies, chunks, rows, size, group), streams, slots
        ),
        out_shape=jax.ShapeDtypeStruct(block, BF16),
        in_specs=[vmem] * 3,
        out_specs=vmem,
        scratch_shapes=[
            pltpu.VMEM(block, BF16),
            pltpu.VMEM((2,) + block, BF16),
            pltpu.VMEM((relayed,) + block[1:], BF16),
            pltpu.VMEM((energies, 2, 2 * size, 2 * size), BF16),
            pltpu.VMEM((energies, 2, chunks // group, size, 2 * group * rows), BF16),
            pltpu.VMEM((2 * size, 2 * size), BF16),
            pltpu.VMEM((energies, size, 2 * size), F32),
            sem((energies, chunks)),
            sem((2, energies, chunks)),
            sem((relayed, chunks)),
            sem((energies, chunks)),
            sem((2, energies, chunks)),
            sem((relayed, chunks)),
        ],
        compiler_params=pltpu.CompilerParams(
            collective_id=0, has_side_effects=True, vmem_limit_bytes=48 * 2**20
        ),
        name="sweep",
    )(
        green_local.reshape(block),
        hopping.reshape(size, 2 * size),
        coupling.reshape(size, size),
    )
    return result.reshape(green_local.shape)


def square_kernel(
    dims,
    g_ref, h_ref, c_ref, out_ref,
    own, fin, halo, res, back, hop_in, cpl_in, right, left, hops, cpl, total,
    fin_sem, halo_sem, back_sem, g_sem, hop_sem, cpl_sem,
    fin_send, halo_send, back_send, g_send, hop_send, cpl_send,
):
    rows_of, chunks, rows, size, group = dims
    blocks, deep = chunks // group, group * rows
    parts_of_half = hop_in.shape[1]
    me = lax.axis_index("layer")
    d = lax.axis_index("energy")
    has_low, has_high = d > 0, d < rows_of - 1
    half = lax.rem(d, 2)
    twin = d + 1 - 2 * half
    first, even, odd, last = me == 3, me == 1, me == 2, me == 0
    ends, middle = first | last, even | odd

    barrier = pltpu.get_barrier_semaphore()
    count = has_low.astype(jnp.int32) + has_high.astype(jnp.int32)
    for l, partners in enumerate(((1, 2), (0, 2, 3), (0, 1, 3), (1, 2))):
        @pl.when(me == l)
        def _(partners=partners):
            for other in partners:
                pl.semaphore_signal(barrier, inc=1, device_id={"layer": other}, device_id_type=MESH)

        count = count + jnp.where(me == l, len(partners), 0)

    @pl.when(has_low)
    def _():
        pl.semaphore_signal(barrier, inc=1, device_id={"energy": d - 1}, device_id_type=MESH)

    @pl.when(has_high)
    def _():
        pl.semaphore_signal(barrier, inc=1, device_id={"energy": d + 1}, device_id_type=MESH)

    pl.semaphore_wait(barrier, count)

    def remote(src, dst, send, recv, **where):
        return pltpu.make_async_remote_copy(
            src_ref=src, dst_ref=dst, send_sem=send, recv_sem=recv,
            device_id=where, device_id_type=MESH,
        )

    def halo_copy(src, side, slot, c):
        return remote(
            src, halo.at[side, slot, c], halo_send.at[side, slot, c], halo_sem.at[side, slot, c],
            energy=d + 1 if side == 0 else d - 1,
        )

    def forward(src, slot, c):
        @pl.when(has_high)
        def _():
            halo_copy(src, 0, slot, c).start()

        @pl.when(has_low)
        def _():
            halo_copy(src, 1, slot, c).start()

    def result_copy(k, c, target, slot):
        return remote(
            res.at[k, c], fin.at[slot, c], fin_send.at[k, c], fin_sem.at[slot, c], layer=target
        )

    def back_copy(k, c, target):
        return remote(res.at[k, c], back.at[c], back_send.at[c], back_sem.at[c], layer=target)

    def block_copy(i, k, target):
        return remote(g_ref.at[i], own.at[k], g_send, g_sem, layer=target)

    def hop_copy(src, stage, side, q, **where):
        return remote(
            src.at[side, q], hop_in.at[side, q], hop_send.at[stage, q], hop_sem.at[side, q], **where
        )

    def cpl_copy(src, stage, side, **where):
        return remote(src.at[side], cpl_in.at[side], cpl_send.at[stage], cpl_sem.at[side], **where)

    def factors_to(target):
        cpl_copy(c_ref, 0, half, layer=target).start()
        for q in range(parts_of_half):
            hop_copy(h_ref, 0, half, q, layer=target).start()

    @pl.when(first)
    def _():
        def body(c, carry):
            for k in range(2):
                forward(g_ref.at[k, c], k, c)
            return carry

        lax.fori_loop(0, chunks, body, 0)
        fin[...] = g_ref[...]

    @pl.when(odd)
    def _():
        block_copy(0, 0, 1).start()
        factors_to(0)
        own[0] = g_ref[1]

    @pl.when(even)
    def _():
        factors_to(2)
        block_copy(1, 1, 2).start()
        own[1] = g_ref[0]

    @pl.when(ends)
    def _():
        own[...] = g_ref[...]

    @pl.when(d == 0)
    def _():
        halo[0] = jnp.zeros_like(halo[0])

    @pl.when(d == rows_of - 1)
    def _():
        halo[1] = jnp.zeros_like(halo[1])

    @pl.when(last)
    def _():
        cpl_copy(cpl_in, 0, half, layer=1).wait_recv()
        cpl_copy(cpl_in, 0, half, layer=1).start()
        for q in range(parts_of_half):
            hop_copy(hop_in, 0, half, q, layer=1).wait_recv()
            hop_copy(hop_in, 0, half, q, layer=1).start()

    def swap_halves():
        cpl_copy(cpl_in, 1, half, energy=twin).wait_recv()
        cpl_copy(cpl_in, 1, half, energy=twin).start()
        for q in range(parts_of_half):
            hop_copy(hop_in, 1, half, q, energy=twin).wait_recv()
            hop_copy(hop_in, 1, half, q, energy=twin).start()
        cpl_copy(cpl_in, 1, 1 - half, energy=twin).wait_recv()
        for q in range(parts_of_half):
            hop_copy(hop_in, 1, 1 - half, q, energy=twin).wait_recv()

    def prepare(k, arrived):
        def fill(hop_src, cpl_src):
            whole = hop_src[...].reshape(size, 2 * size)
            hops[:size, :] = whole
            hops[size:, :size] = -whole[:, size:]
            hops[size:, size:] = whole[:, :size]
            cpl[...] = cpl_src[...].reshape(size, size)

        @pl.when(arrived)
        def _():
            block_copy(0, k, 1).wait_recv()
            fill(hop_in, cpl_in)

        @pl.when(jnp.logical_not(arrived))
        def _():
            fill(h_ref, c_ref)

        full = own[k].reshape(size, 2 * size)
        total[k] = full.astype(F32)
        coupled = jnp.dot(full, hops[...], preferred_element_type=F32).astype(BF16)
        parts = [coupled[:, :size], coupled[:, size:]]
        for which in range(2):
            if which == 1:
                parts = [
                    jnp.dot(part, cpl[...], preferred_element_type=F32).astype(BF16)
                    for part in parts
                ]
            for j in range(blocks):
                for part in range(2):
                    left[k, which, j, :, part * deep : (part + 1) * deep] = parts[part][
                        :, j * deep : (j + 1) * deep
                    ]
            flip_r, flip_i = parts[0].T, parts[1].T
            right[k, which, :size, :size] = flip_r
            right[k, which, :size, size:] = flip_i
            right[k, which, size:, :size] = -flip_i
            right[k, which, size:, size:] = flip_r

    def prepare_early(n, carry):
        k = jnp.where(even, 1 - n, n)

        @pl.when(even & (n == 1))
        def _():
            swap_halves()

        @pl.when(jnp.logical_not(odd & (n == 1)))
        def _():
            prepare(k, even & (n == 1))

        return carry

    lax.fori_loop(0, 2, prepare_early, 0)

    def add_block(k, which, j, value):
        mid = jnp.dot(value, right[k, which], preferred_element_type=F32).astype(BF16)
        swapped = jnp.concatenate([-mid[:, size:], mid[:, :size]], axis=1)
        both = jnp.concatenate([mid, swapped], axis=0)
        total[k] += jnp.dot(left[k, which, j], both, preferred_element_type=F32)

    def block_of(ref, j):
        return ref[pl.ds(j * group, group)].reshape(deep, 2 * size)

    def arrive(slot, c):
        result_copy(0, c, me, slot).wait_recv()
        forward(fin.at[slot, c], slot, c)

    def add_partner(k, j):
        for sub in range(group):
            c = j * group + sub

            @pl.when(has_low)
            def _(c=c):
                halo_copy(fin.at[k, c], 0, k, c).wait_recv()

            @pl.when(has_high)
            def _(c=c):
                halo_copy(fin.at[k, c], 1, k, c).wait_recv()

        partner = block_of(halo.at[0, k], j).astype(F32) + block_of(halo.at[1, k], j).astype(F32)
        add_block(k, 1, j, partner.astype(BF16))

    def round_chunk(k, c):
        res[k, c] = total[k, pl.ds(pl.multiple_of(c * rows, 16), rows), :].astype(BF16)

    @pl.when(ends)
    def _():
        def step(t, carry):
            @pl.when((t < blocks) & last)
            def _():
                for sub in range(group):
                    for k in range(2):
                        arrive(k, t * group + sub)

            for k in range(2):
                @pl.when(t < blocks)
                def _(k=k):
                    add_block(k, 0, t, block_of(fin.at[k], t))

            for k in range(2):
                @pl.when(t >= 1)
                def _(k=k):
                    add_partner(k, t - 1)

            return carry

        lax.fori_loop(0, blocks + 1, step, 0)

        def finish(c, carry):
            for k in range(2):
                round_chunk(k, c)

                @pl.when(first)
                def _(k=k):
                    result_copy(k, c, 1 + k, 0).start()
            return carry

        lax.fori_loop(0, chunks, finish, 0)
        out_ref[...] = res[...]

    @pl.when(middle)
    def _():
        @pl.when(odd)
        def _():
            swap_halves()

        def step(t, carry):
            @pl.when(t < blocks)
            def _():
                for sub in range(group):
                    arrive(0, t * group + sub)
                add_block(0, 0, t, block_of(fin.at[0], t))

            @pl.when(t >= 1)
            def _():
                add_partner(0, t - 1)

            return carry

        lax.fori_loop(0, blocks + 1, step, 0)

        def finish_two(c, carry):
            round_chunk(0, c)
            forward(res.at[0, c], 1, c)
            return carry

        lax.fori_loop(0, chunks, finish_two, 0)

        @pl.when(even)
        def _():
            def body(c, carry):
                back_copy(0, c, 2).start()
                return carry

            lax.fori_loop(0, chunks, body, 0)

        @pl.when(odd)
        def _():
            prepare(1, odd)

        def near(j, carry):
            add_block(1, 0, j, block_of(res.at[0], j))
            return carry

        def far(j, carry):
            add_partner(1, j)
            return carry

        lax.fori_loop(0, blocks, near, 0)
        lax.fori_loop(0, blocks, far, 0)

        def finish_one(c, carry):
            round_chunk(1, c)
            result_copy(1, c, 0, me - 1).start()
            return carry

        lax.fori_loop(0, chunks, finish_one, 0)

        @pl.when(odd)
        def _():
            def body(c, carry):
                back_copy(1, c, 1).start()
                return carry

            lax.fori_loop(0, chunks, body, 0)
            out_ref[1] = res[0]

        @pl.when(even)
        def _():
            out_ref[0] = res[1]

        def home(c, carry):
            back_copy(0, c, me).wait_recv()
            out_ref[2 - me, c] = back[c]
            return carry

        lax.fori_loop(0, chunks, home, 0)

    def drain(c, carry):
        for k in range(2):
            @pl.when(first | (middle & (k == 1)))
            def _(k=k):
                result_copy(k, c, me, 0).wait_send()

            @pl.when(has_high)
            def _(k=k):
                halo_copy(fin.at[k, c], 0, k, c).wait_send()

            @pl.when(has_low)
            def _(k=k):
                halo_copy(fin.at[k, c], 1, k, c).wait_send()

        @pl.when(middle)
        def _():
            back_copy(0, c, me).wait_send()

        return carry

    lax.fori_loop(0, chunks, drain, 0)

    @pl.when(middle)
    def _():
        block_copy(0, 0, me).wait_send()
        cpl_copy(cpl_in, 1, half, energy=twin).wait_send()
        for q in range(parts_of_half):
            hop_copy(hop_in, 1, half, q, energy=twin).wait_send()

    @pl.when(middle | last)
    def _():
        cpl_copy(cpl_in, 0, half, layer=me).wait_send()
        for q in range(parts_of_half):
            hop_copy(hop_in, 0, half, q, layer=me).wait_send()


def square_sweep(green_local, hopping, coupling):
    _, _, size, _, _ = green_local.shape
    rows_of = lax.axis_size("energy")
    rows = 32
    chunks, group = size // rows, 128 // rows
    block = (2, chunks, rows, 2 * size)
    hop_block = (2, 2, size // 4, 2 * size)
    cpl_block = (2, size // 2, size)
    sem = pltpu.SemaphoreType.DMA
    vmem = pl.BlockSpec(memory_space=pltpu.VMEM)
    result = pl.pallas_call(
        functools.partial(square_kernel, (rows_of, chunks, rows, size, group)),
        out_shape=jax.ShapeDtypeStruct(block, BF16),
        in_specs=[vmem] * 3,
        out_specs=vmem,
        scratch_shapes=[
            pltpu.VMEM(block, BF16),
            pltpu.VMEM(block, BF16),
            pltpu.VMEM((2,) + block, BF16),
            pltpu.VMEM(block, BF16),
            pltpu.VMEM(block[1:], BF16),
            pltpu.VMEM(hop_block, BF16),
            pltpu.VMEM(cpl_block, BF16),
            pltpu.VMEM((2, 2, 2 * size, 2 * size), BF16),
            pltpu.VMEM((2, 2, chunks // group, size, 2 * group * rows), BF16),
            pltpu.VMEM((2 * size, 2 * size), BF16),
            pltpu.VMEM((size, size), BF16),
            pltpu.VMEM((2, size, 2 * size), F32),
            sem((2, chunks)),
            sem((2, 2, chunks)),
            sem((chunks,)),
            sem,
            sem(hop_block[:2]),
            sem((2,)),
            sem((2, chunks)),
            sem((2, 2, chunks)),
            sem((chunks,)),
            sem,
            sem((2, hop_block[1])),
            sem((2,)),
        ],
        compiler_params=pltpu.CompilerParams(
            collective_id=1, has_side_effects=True, vmem_limit_bytes=48 * 2**20
        ),
        name="square_sweep",
    )(
        green_local.reshape(block),
        hopping.reshape(hop_block),
        coupling.reshape(cpl_block),
    )
    return result.reshape(green_local.shape)


def solution(mesh):
    def step(green_local, hopping, coupling):
        layers, rows_of = lax.axis_size("layer"), lax.axis_size("energy")
        _, energies, size, _, _ = green_local.shape
        square = layers == 4 and energies == 2 and rows_of % 2 == 0 and size % 128 == 0
        return (square_sweep if square else per_device)(green_local, hopping, coupling)

    placed = (
        P("layer", "energy", None, None, None),
        P("layer", None, None, None),
        P("layer", None, None),
    )
    return jax.shard_map(
        step,
        mesh=mesh,
        in_specs=placed,
        out_specs=P("layer", "energy", None, None, None),
        check_vma=False,
    )
```

```python
import functools

import jax
import jax.numpy as jnp
from jax import lax
from jax.experimental import pallas as pl
from jax.experimental.pallas import tpu as pltpu
from jax.sharding import PartitionSpec as P

MESH = pl.DeviceIdType.MESH
F32 = jnp.float32
BF16 = jnp.bfloat16


def routes(layers, energies, chunks):
    return [(i, 0, chunks, (l, l - 1)) for l in range(layers - 1, 0, -1) for i in range(energies)]


def kernel(
    dims, streams, slots,
    g_ref, h_ref, c_ref, out_ref,
    fin, halo, relay, right, left, hops, total,
    fin_sem, halo_sem, relay_sem, out_send, halo_send, relay_send,
):
    layers, rows_of, energies, chunks, rows, size, group = dims
    blocks, deep = chunks // group, group * rows
    me = lax.axis_index("layer")
    d = lax.axis_index("energy")
    has_low, has_high = d > 0, d < rows_of - 1
    top = me == layers - 1

    pairs = sorted({tuple(sorted(p)) for _, _, _, path in streams for p in zip(path, path[1:])})
    barrier = pltpu.get_barrier_semaphore()
    count = has_low.astype(jnp.int32) + has_high.astype(jnp.int32)
    for l in range(layers):
        partners = [b if a == l else a for a, b in pairs if l in (a, b)]

        @pl.when(me == l)
        def _(partners=partners):
            for other in partners:
                pl.semaphore_signal(barrier, inc=1, device_id={"layer": other}, device_id_type=MESH)

        count = count + jnp.where(me == l, len(partners), 0)

    @pl.when(has_low)
    def _():
        pl.semaphore_signal(barrier, inc=1, device_id={"energy": d - 1}, device_id_type=MESH)

    @pl.when(has_high)
    def _():
        pl.semaphore_signal(barrier, inc=1, device_id={"energy": d + 1}, device_id_type=MESH)

    pl.semaphore_wait(barrier, count)

    def halo_copy(src, side, i, c):
        return pltpu.make_async_remote_copy(
            src_ref=src.at[i, c], dst_ref=halo.at[side, i, c],
            send_sem=halo_send.at[side, i, c], recv_sem=halo_sem.at[side, i, c],
            device_id={"energy": d + 1 if side == 0 else d - 1}, device_id_type=MESH,
        )

    def forward(src, i, c):
        @pl.when(has_high)
        def _():
            halo_copy(src, 0, i, c).start()

        @pl.when(has_low)
        def _():
            halo_copy(src, 1, i, c).start()

    def stream_copy(s, hop, c):
        i, _, _, path = streams[s]
        target = path[hop + 1]
        if hop == 0:
            src, send = out_ref.at[i, c], out_send.at[i, c]
        else:
            src, send = relay.at[slots[s], c], relay_send.at[slots[s], c]
        if hop == len(path) - 2:
            dst, recv = fin.at[i, c], fin_sem.at[i, c]
        else:
            dst, recv = relay.at[slots[s], c], relay_sem.at[slots[s], c]
        return pltpu.make_async_remote_copy(
            src_ref=src, dst_ref=dst, send_sem=send, recv_sem=recv,
            device_id={"layer": target}, device_id_type=MESH,
        )

    def pass_on(s, hop):
        def body(c, carry):
            stream_copy(s, hop - 1, c).wait_recv()
            stream_copy(s, hop, c).start()
            return carry

        lax.fori_loop(streams[s][1], streams[s][2], body, 0)

    @pl.when(top)
    def _():
        def body(c, carry):
            for i in range(energies):
                forward(g_ref, i, c)
            return carry

        lax.fori_loop(0, chunks, body, 0)
        fin[...] = g_ref[...]

    @pl.when(d == 0)
    def _():
        halo[0] = jnp.zeros_like(halo[0])

    @pl.when(d == rows_of - 1)
    def _():
        halo[1] = jnp.zeros_like(halo[1])

    hop_r, hop_i = h_ref[:, :size], h_ref[:, size:]
    hops[:size, :] = h_ref[...]
    hops[size:, :size] = -hop_i
    hops[size:, size:] = hop_r
    for i in range(energies):
        full = g_ref[i].reshape(size, 2 * size)
        total[i] = full.astype(F32)
        coupled = jnp.dot(full, hops[...], preferred_element_type=F32).astype(BF16)
        parts = [coupled[:, :size], coupled[:, size:]]
        for which in range(2):
            if which == 1:
                parts = [
                    jnp.dot(part, c_ref[...], preferred_element_type=F32).astype(BF16)
                    for part in parts
                ]
            for j in range(blocks):
                for part in range(2):
                    left[i, which, j, :, part * deep : (part + 1) * deep] = parts[part][
                        :, j * deep : (j + 1) * deep
                    ]
            flip_r, flip_i = parts[0].T, parts[1].T
            right[i, which, :size, :size] = flip_r
            right[i, which, :size, size:] = flip_i
            right[i, which, size:, :size] = -flip_i
            right[i, which, size:, size:] = flip_r

    def relays(when):
        for l in range(layers):
            jobs = [
                (s, hop)
                for s, (_, _, _, path) in enumerate(streams)
                for hop, node in enumerate(path[1:-1], 1)
                if node == l and (path[0] > l + 1 if when == "before" else path[0] <= l)
            ]
            if jobs:
                @pl.when(me == l)
                def _(jobs=jobs):
                    for s, hop in jobs:
                        pass_on(s, hop)

    relays("before")

    def add_block(i, which, j, value):
        mid = jnp.dot(value, right[i, which], preferred_element_type=F32).astype(BF16)
        swapped = jnp.concatenate([-mid[:, size:], mid[:, :size]], axis=1)
        both = jnp.concatenate([mid, swapped], axis=0)
        total[i] += jnp.dot(left[i, which, j], both, preferred_element_type=F32)

    def block_of(ref, j):
        return ref[pl.ds(j * group, group)].reshape(deep, 2 * size)

    lags = []
    for i in range(energies):
        lag = jnp.int32(0)
        for l in range(layers - 1):
            hops_of = {e: len(path) for e, lo, _, path in streams if path[-1] == l and lo == 0}
            late = 1 if hops_of[i] > min(hops_of.values()) else 0
            lag = lag + jnp.where(me == l, late, 0)
        lags.append(lag)
    worst = 1 if any(len(path) > 2 for _, _, _, path in streams) else 0

    def step(t, carry):
        for sub in range(group):
            for i in range(energies):
                j = t - lags[i]

                @pl.when((j >= 0) & (j < blocks) & jnp.logical_not(top))
                def _(i=i, j=j, sub=sub):
                    c = j * group + sub
                    pltpu.make_async_remote_copy(
                        src_ref=fin.at[i, c], dst_ref=fin.at[i, c],
                        send_sem=out_send.at[i, c], recv_sem=fin_sem.at[i, c],
                        device_id={"layer": me + 1}, device_id_type=MESH,
                    ).wait_recv()
                    forward(fin, i, c)

        for i in range(energies):
            j = t - lags[i]

            @pl.when((j >= 0) & (j < blocks))
            def _(i=i, j=j):
                add_block(i, 0, j, block_of(fin.at[i], j))

        for i in range(energies):
            j = t - lags[i] - 1

            @pl.when((j >= 0) & (j < blocks))
            def _(i=i, j=j):
                for sub in range(group):
                    @pl.when(has_low)
                    def _(sub=sub):
                        halo_copy(fin, 0, i, j * group + sub).wait_recv()

                    @pl.when(has_high)
                    def _(sub=sub):
                        halo_copy(fin, 1, i, j * group + sub).wait_recv()

                partner = block_of(halo.at[0, i], j).astype(F32) + block_of(
                    halo.at[1, i], j
                ).astype(F32)
                add_block(i, 1, j, partner.astype(BF16))

        return carry

    lax.fori_loop(0, blocks + 1 + worst, step, 0)

    def finish(c, carry):
        for i in reversed(range(energies)):
            out_ref[i, c] = total[i, pl.ds(pl.multiple_of(c * rows, 16), rows), :].astype(BF16)
            for s, (e, first, end, path) in enumerate(streams):
                if e == i:
                    @pl.when((me == path[0]) & (c >= first) & (c < end))
                    def _(s=s):
                        stream_copy(s, 0, c).start()
        return carry

    lax.fori_loop(0, chunks, finish, 0)
    relays("after")

    def drain(c, carry):
        for s, (_, first, end, path) in enumerate(streams):
            for hop, node in enumerate(path[:-1]):
                @pl.when((me == node) & (c >= first) & (c < end))
                def _(s=s, hop=hop):
                    stream_copy(s, hop, c).wait_send()
        for i in range(energies):
            @pl.when(has_high)
            def _(i=i):
                halo_copy(fin, 0, i, c).wait_send()

            @pl.when(has_low)
            def _(i=i):
                halo_copy(fin, 1, i, c).wait_send()
        return carry

    lax.fori_loop(0, chunks, drain, 0)


def per_device(green_local, hopping, coupling):
    _, energies, size, _, _ = green_local.shape
    layers, rows_of = lax.axis_size("layer"), lax.axis_size("energy")
    rows = 32 if size % 32 == 0 else 16
    chunks = size // rows
    group = 128 // rows if size % 128 == 0 else 1
    streams = routes(layers, energies, chunks)
    slots, relayed = {}, 0
    for s, (_, _, _, path) in enumerate(streams):
        if len(path) > 2:
            slots[s] = relayed
            relayed += 1
    relayed = max(relayed, 1)
    block = (energies, chunks, rows, 2 * size)
    sem = pltpu.SemaphoreType.DMA
    vmem = pl.BlockSpec(memory_space=pltpu.VMEM)
    result = pl.pallas_call(
        functools.partial(
            kernel, (layers, rows_of, energies, chunks, rows, size, group), streams, slots
        ),
        out_shape=jax.ShapeDtypeStruct(block, BF16),
        in_specs=[vmem] * 3,
        out_specs=vmem,
        scratch_shapes=[
            pltpu.VMEM(block, BF16),
            pltpu.VMEM((2,) + block, BF16),
            pltpu.VMEM((relayed,) + block[1:], BF16),
            pltpu.VMEM((energies, 2, 2 * size, 2 * size), BF16),
            pltpu.VMEM((energies, 2, chunks // group, size, 2 * group * rows), BF16),
            pltpu.VMEM((2 * size, 2 * size), BF16),
            pltpu.VMEM((energies, size, 2 * size), F32),
            sem((energies, chunks)),
            sem((2, energies, chunks)),
            sem((relayed, chunks)),
            sem((energies, chunks)),
            sem((2, energies, chunks)),
            sem((relayed, chunks)),
        ],
        compiler_params=pltpu.CompilerParams(
            collective_id=0, has_side_effects=True, vmem_limit_bytes=48 * 2**20
        ),
        name="sweep",
    )(
        green_local.reshape(block),
        hopping.reshape(size, 2 * size),
        coupling.reshape(size, size),
    )
    return result.reshape(green_local.shape)


def square_kernel(
    dims,
    g_ref, h_ref, c_ref, out_ref,
    own, fin, halo, res, back, hop_in, cpl_in, right, left, hops, cpl, mid, total,
    fin_sem, halo_sem, back_sem, g_sem, hop_sem, cpl_sem,
    fin_send, halo_send, back_send, g_send, hop_send, cpl_send,
):
    rows_of, chunks, rows, size, group = dims
    blocks, deep = chunks // group, group * rows
    parts_of_half = 2
    hop_rows = size // (2 * parts_of_half)
    me = lax.axis_index("layer")
    d = lax.axis_index("energy")
    has_low, has_high = d > 0, d < rows_of - 1
    half = lax.rem(d, 2)
    twin = d + 1 - 2 * half
    first, even, odd, last = me == 3, me == 1, me == 2, me == 0
    ends, middle = first | last, even | odd

    barrier = pltpu.get_barrier_semaphore()
    count = has_low.astype(jnp.int32) + has_high.astype(jnp.int32)
    for l, partners in enumerate(((1, 2), (0, 2, 3), (0, 1, 3), (1, 2))):
        @pl.when(me == l)
        def _(partners=partners):
            for other in partners:
                pl.semaphore_signal(barrier, inc=1, device_id={"layer": other}, device_id_type=MESH)

        count = count + jnp.where(me == l, len(partners), 0)

    @pl.when(has_low)
    def _():
        pl.semaphore_signal(barrier, inc=1, device_id={"energy": d - 1}, device_id_type=MESH)

    @pl.when(has_high)
    def _():
        pl.semaphore_signal(barrier, inc=1, device_id={"energy": d + 1}, device_id_type=MESH)

    pl.semaphore_wait(barrier, count)

    def remote(src, dst, send, recv, **where):
        return pltpu.make_async_remote_copy(
            src_ref=src, dst_ref=dst, send_sem=send, recv_sem=recv,
            device_id=where, device_id_type=MESH,
        )

    def halo_copy(src, side, slot, c):
        return remote(
            src, halo.at[side, slot, c], halo_send.at[side, slot, c], halo_sem.at[side, slot, c],
            energy=d + 1 if side == 0 else d - 1,
        )

    def forward(src, slot, c):
        @pl.when(has_high)
        def _():
            halo_copy(src, 0, slot, c).start()

        @pl.when(has_low)
        def _():
            halo_copy(src, 1, slot, c).start()

    def result_copy(k, c, target, slot):
        return remote(
            res.at[k, c], fin.at[slot, c], fin_send.at[k, c], fin_sem.at[slot, c], layer=target
        )

    def back_copy(k, c, target):
        return remote(res.at[k, c], back.at[c], back_send.at[c], back_sem.at[c], layer=target)

    def block_copy(i, k, target):
        return remote(g_ref.at[i], own.at[k], g_send, g_sem, layer=target)

    def hop_copy(src, stage, side, q, **where):
        start = pl.multiple_of((side * parts_of_half + q) * hop_rows, 16)
        part = pl.ds(start, hop_rows)
        return remote(
            src.at[part], hop_in.at[part], hop_send.at[stage, q], hop_sem.at[side, q], **where
        )

    def cpl_copy(src, stage, side, **where):
        return remote(src.at[side], cpl_in.at[side], cpl_send.at[stage], cpl_sem.at[side], **where)

    def factors_to(target):
        cpl_copy(c_ref, 0, half, layer=target).start()
        for q in range(parts_of_half):
            hop_copy(h_ref, 0, half, q, layer=target).start()

    @pl.when(first)
    def _():
        def body(c, carry):
            for k in range(2):
                forward(g_ref.at[k, c], k, c)
            return carry

        lax.fori_loop(0, chunks, body, 0)
        fin[...] = g_ref[...]

    @pl.when(odd)
    def _():
        block_copy(0, 0, 1).start()
        factors_to(0)
        own[0] = g_ref[1]

    @pl.when(even)
    def _():
        factors_to(2)
        block_copy(1, 1, 2).start()
        own[1] = g_ref[0]

    @pl.when(ends)
    def _():
        own[...] = g_ref[...]

    @pl.when(d == 0)
    def _():
        halo[0] = jnp.zeros_like(halo[0])

    @pl.when(d == rows_of - 1)
    def _():
        halo[1] = jnp.zeros_like(halo[1])

    @pl.when(last)
    def _():
        cpl_copy(cpl_in, 0, half, layer=1).wait_recv()
        cpl_copy(cpl_in, 0, half, layer=1).start()
        for q in range(parts_of_half):
            hop_copy(hop_in, 0, half, q, layer=1).wait_recv()
            hop_copy(hop_in, 0, half, q, layer=1).start()

    def swap_halves():
        cpl_copy(cpl_in, 1, half, energy=twin).wait_recv()
        cpl_copy(cpl_in, 1, half, energy=twin).start()
        for q in range(parts_of_half):
            hop_copy(hop_in, 1, half, q, energy=twin).wait_recv()
            hop_copy(hop_in, 1, half, q, energy=twin).start()
        cpl_copy(cpl_in, 1, 1 - half, energy=twin).wait_recv()
        for q in range(parts_of_half):
            hop_copy(hop_in, 1, 1 - half, q, energy=twin).wait_recv()

    def expand(ref, start, value):
        count, low = value.shape[0], start + size
        if not isinstance(start, int):
            start, low = pl.multiple_of(start, 16), pl.multiple_of(low, 16)
        ref[pl.ds(start, count), :] = value
        ref[pl.ds(low, count), :size] = -value[:, size:]
        ref[pl.ds(low, count), size:] = value[:, :size]

    def prepare(k, arrived):
        def fill(hop_src, cpl_src):
            expand(hops, 0, hop_src[...])
            cpl[...] = cpl_src[...].reshape(size, size)

        @pl.when(arrived)
        def _():
            block_copy(0, k, 1).wait_recv()
            fill(hop_in, cpl_in)

        @pl.when(jnp.logical_not(arrived))
        def _():
            fill(h_ref, c_ref)

        full = own[k].reshape(size, 2 * size)
        coupled = jnp.dot(full, hops[...], preferred_element_type=F32).astype(BF16)
        parts = [coupled[:, :size], coupled[:, size:]]
        for which in range(2):
            if which == 1:
                parts = [
                    jnp.dot(part, cpl[...], preferred_element_type=F32).astype(BF16)
                    for part in parts
                ]
            for part in range(2):
                left[k, which, :, part * size : (part + 1) * size] = parts[part]
            flip_r, flip_i = parts[0].T, parts[1].T
            right[k, which, :size, :size] = flip_r
            right[k, which, :size, size:] = flip_i
            right[k, which, size:, :size] = -flip_i
            right[k, which, size:, size:] = flip_r

    def prepare_early(n, carry):
        k = jnp.where(even, 1 - n, n)

        @pl.when(even & (n == 1))
        def _():
            swap_halves()

        @pl.when(jnp.logical_not(odd & (n == 1)))
        def _():
            prepare(k, even & (n == 1))

        return carry

    lax.fori_loop(0, 2, prepare_early, 0)

    def near(k, ref):
        value = jnp.dot(
            ref[...].reshape(size, 2 * size), right[k, 0], preferred_element_type=F32
        ).astype(BF16)
        expand(hops, 0, value)
        total[k] = own[k].reshape(size, 2 * size).astype(F32) + jnp.dot(
            left[k, 0], hops[...], preferred_element_type=F32
        )

    def close(k):
        value = total[k] + jnp.dot(left[k, 1], mid[k], preferred_element_type=F32)
        res[k] = value.astype(BF16).reshape(chunks, rows, 2 * size)

    def block_of(ref, j):
        return ref[pl.ds(j * group, group)].reshape(deep, 2 * size)

    def arrive(slot, c):
        result_copy(0, c, me, slot).wait_recv()
        forward(fin.at[slot, c], slot, c)

    def add_partner(k, j):
        for sub in range(group):
            c = j * group + sub

            @pl.when(has_low)
            def _(c=c):
                halo_copy(fin.at[k, c], 0, k, c).wait_recv()

            @pl.when(has_high)
            def _(c=c):
                halo_copy(fin.at[k, c], 1, k, c).wait_recv()

        partner = block_of(halo.at[0, k], j).astype(F32) + block_of(halo.at[1, k], j).astype(F32)
        value = jnp.dot(partner.astype(BF16), right[k, 1], preferred_element_type=F32)
        expand(mid.at[k], j * deep, value.astype(BF16))

    @pl.when(ends)
    def _():
        @pl.when(first)
        def _():
            for k in range(2):
                near(k, fin.at[k])

        def step(t, carry):
            @pl.when((t < blocks) & last)
            def _():
                for sub in range(group):
                    for k in range(2):
                        arrive(k, t * group + sub)

            @pl.when((t == blocks) & last)
            def _():
                for k in range(2):
                    near(k, fin.at[k])

            @pl.when(t >= 1)
            def _():
                for k in range(2):
                    add_partner(k, t - 1)

            return carry

        lax.fori_loop(0, blocks + 1, step, 0)

        for k in range(2):
            close(k)

            @pl.when(first)
            def _(k=k):
                def body(c, carry):
                    result_copy(k, c, 1 + k, 0).start()
                    return carry

                lax.fori_loop(0, chunks, body, 0)

        out_ref[...] = res[...]

    @pl.when(middle)
    def _():
        @pl.when(odd)
        def _():
            swap_halves()

        def step(t, carry):
            @pl.when(t < blocks)
            def _():
                for sub in range(group):
                    arrive(0, t * group + sub)

            @pl.when(t == blocks)
            def _():
                near(0, fin.at[0])

            @pl.when(t >= 1)
            def _():
                add_partner(0, t - 1)

            return carry

        lax.fori_loop(0, blocks + 1, step, 0)

        close(0)

        def finish_two(c, carry):
            forward(res.at[0, c], 1, c)
            return carry

        lax.fori_loop(0, chunks, finish_two, 0)

        @pl.when(even)
        def _():
            def body(c, carry):
                back_copy(0, c, 2).start()
                return carry

            lax.fori_loop(0, chunks, body, 0)

        @pl.when(odd)
        def _():
            prepare(1, odd)

        near(1, res.at[0])

        def far(j, carry):
            add_partner(1, j)
            return carry

        lax.fori_loop(0, blocks, far, 0)
        close(1)

        def finish_one(c, carry):
            result_copy(1, c, 0, me - 1).start()
            return carry

        lax.fori_loop(0, chunks, finish_one, 0)

        @pl.when(odd)
        def _():
            def body(c, carry):
                back_copy(1, c, 1).start()
                return carry

            lax.fori_loop(0, chunks, body, 0)
            out_ref[1] = res[0]

        @pl.when(even)
        def _():
            out_ref[0] = res[1]

        def home(c, carry):
            back_copy(0, c, me).wait_recv()
            out_ref[2 - me, c] = back[c]
            return carry

        lax.fori_loop(0, chunks, home, 0)

    def drain(c, carry):
        for k in range(2):
            @pl.when(first | (middle & (k == 1)))
            def _(k=k):
                result_copy(k, c, me, 0).wait_send()

            @pl.when(has_high)
            def _(k=k):
                halo_copy(fin.at[k, c], 0, k, c).wait_send()

            @pl.when(has_low)
            def _(k=k):
                halo_copy(fin.at[k, c], 1, k, c).wait_send()

        @pl.when(middle)
        def _():
            back_copy(0, c, me).wait_send()

        return carry

    lax.fori_loop(0, chunks, drain, 0)

    @pl.when(middle)
    def _():
        block_copy(0, 0, me).wait_send()
        cpl_copy(cpl_in, 1, half, energy=twin).wait_send()
        for q in range(parts_of_half):
            hop_copy(hop_in, 1, half, q, energy=twin).wait_send()

    @pl.when(middle | last)
    def _():
        cpl_copy(cpl_in, 0, half, layer=me).wait_send()
        for q in range(parts_of_half):
            hop_copy(hop_in, 0, half, q, layer=me).wait_send()


def square_sweep(green_local, hopping, coupling):
    _, _, size, _, _ = green_local.shape
    rows_of = lax.axis_size("energy")
    rows = 32
    chunks, group = size // rows, 128 // rows
    block = (2, chunks, rows, 2 * size)
    hop_block = (size, 2 * size)
    cpl_block = (2, size // 2, size)
    sem = pltpu.SemaphoreType.DMA
    vmem = pl.BlockSpec(memory_space=pltpu.VMEM)
    result = pl.pallas_call(
        functools.partial(square_kernel, (rows_of, chunks, rows, size, group)),
        out_shape=jax.ShapeDtypeStruct(block, BF16),
        in_specs=[vmem] * 3,
        out_specs=vmem,
        scratch_shapes=[
            pltpu.VMEM(block, BF16),
            pltpu.VMEM(block, BF16),
            pltpu.VMEM((2,) + block, BF16),
            pltpu.VMEM(block, BF16),
            pltpu.VMEM(block[1:], BF16),
            pltpu.VMEM(hop_block, BF16),
            pltpu.VMEM(cpl_block, BF16),
            pltpu.VMEM((2, 2, 2 * size, 2 * size), BF16),
            pltpu.VMEM((2, 2, size, 2 * size), BF16),
            pltpu.VMEM((2 * size, 2 * size), BF16),
            pltpu.VMEM((size, size), BF16),
            pltpu.VMEM((2, 2 * size, 2 * size), BF16),
            pltpu.VMEM((2, size, 2 * size), F32),
            sem((2, chunks)),
            sem((2, 2, chunks)),
            sem((chunks,)),
            sem,
            sem((2, 2)),
            sem((2,)),
            sem((2, chunks)),
            sem((2, 2, chunks)),
            sem((chunks,)),
            sem,
            sem((2, 2)),
            sem((2,)),
        ],
        compiler_params=pltpu.CompilerParams(
            collective_id=1, has_side_effects=True, vmem_limit_bytes=48 * 2**20
        ),
        name="square_sweep",
    )(
        green_local.reshape(block),
        hopping.reshape(hop_block),
        coupling.reshape(cpl_block),
    )
    return result.reshape(green_local.shape)


def solution(mesh):
    def step(green_local, hopping, coupling):
        layers, rows_of = lax.axis_size("layer"), lax.axis_size("energy")
        _, energies, size, _, _ = green_local.shape
        square = layers == 4 and energies == 2 and rows_of % 2 == 0 and size % 128 == 0
        return (square_sweep if square else per_device)(green_local, hopping, coupling)

    placed = (
        P("layer", "energy", None, None, None),
        P("layer", None, None, None),
        P("layer", None, None),
    )
    return jax.shard_map(
        step,
        mesh=mesh,
        in_specs=placed,
        out_specs=P("layer", "energy", None, None, None),
        check_vma=False,
    )
```
